256 devices in a mesh: rep: 4 (over x), fsdp: 64 (over z, y, core).
Axes of the slice: x: 4, y: 4, z: 8, core: 2. Of those that a mesh axis runs over, the one named last changes fastest.
Arguments:
- gradient: bfloat16 [192, 512, 512], P(None, 'fsdp'), may hold values from -10 to 10
- block_group: int32 [192], replicated, may hold values from 0 to 3, as said below
- block_owner: int32 [192], replicated, may hold values from 0 to 63, as said below
- left_kronecker: float32 [256, 512, 512], P(('rep', 'fsdp')), may hold values from -6 to 6
- right_kronecker: float32 [256, 512, 512], P(('rep', 'fsdp')), may hold values from -6 to 6
- left_root: bfloat16 [256, 512, 512], P(('rep', 'fsdp'))
- right_root: bfloat16 [256, 512, 512], P(('rep', 'fsdp'))
Outputs:
- new_left: float32 [256, 512, 512], P(('rep', 'fsdp'))
- new_right: float32 [256, 512, 512], P(('rep', 'fsdp'))
- update: bfloat16 [192, 512, 512], P(None, 'fsdp')
The draws below stay inside these ranges and needn't reach their ends.
Inputs may be any that keep to these rules, and one draw needn't show every extreme that they name: `block_group`: together with block_owner, no pair of group and owner is named by more than 1 block, and some pair by exactly 1. `block_owner`: together with block_group, no pair of group and owner is named by more than 1 block, and some pair by exactly 1.
All inputs are finite; a program needn't handle non-finite values.
Results may differ from the reference program's by a relative error of at most 0.0049.
Values may be sent and summed in bfloat16 or wider, within the bound.
A program may use at most 64 MiB of HBM per device.

```python
import math
import jax
import jax.numpy as jnp
from jax import lax

BLOCK_SIDE = 512
SLOTS = 1
NBLK = 192
SLOT_TOTAL_COUNT = 256
N_REP = 4
N_FSDP = 64


def draw_gradient(key, part):
    key = jax.random.fold_in(key, 5)
    key_noise, key_rows, key_cols = jax.random.split(key, 3)
    full_shape = (NBLK, BLOCK_SIDE, BLOCK_SIDE)
    row_part = jax.random.normal(key_rows, (NBLK, BLOCK_SIDE, 1), jnp.float32)
    col_part = jax.random.normal(key_cols, (NBLK, 1, BLOCK_SIDE), jnp.float32)
    noise = jax.random.normal(key_noise, full_shape, jnp.float32)
    mixed = noise + 0.8 * row_part * col_part
    return jnp.clip(mixed, -10.0, 10.0).astype(jnp.bfloat16)


def placement_draw(key):
    slot_total = N_REP * N_FSDP * SLOTS
    key_device, key_rank, key_shuffle = jax.random.split(key, 3)
    chosen_device = jax.random.randint(key_device, (), 0, N_REP * N_FSDP)
    rank_order = jax.random.permutation(key_rank, slot_total).astype(jnp.int32) + 1
    device_of = jnp.arange(slot_total, dtype=jnp.int32) // SLOTS
    scores = jnp.where(device_of == chosen_device, 0, rank_order)
    sorted_order = jnp.argsort(scores, stable=True).astype(jnp.int32)
    picked = sorted_order[:NBLK]
    shuffle = jax.random.permutation(key_shuffle, NBLK)
    return picked[shuffle].astype(jnp.int32)


def draw_block_group(key, part):
    positions = placement_draw(key)
    return (positions // (N_FSDP * SLOTS)).astype(jnp.int32)


def draw_block_owner(key, part):
    positions = placement_draw(key)
    return (positions // SLOTS % N_FSDP).astype(jnp.int32)


def root_matrix(key, spread, upper_end):
    slot_total = N_REP * N_FSDP * SLOTS
    key_diagonal, key_noise = jax.random.split(key)
    diagonal = jnp.exp(jax.random.uniform(key_diagonal, (slot_total, BLOCK_SIDE), jnp.float32, -math.log(upper_end), math.log(upper_end)))
    offdiagonal_noise = jax.random.normal(key_noise, (slot_total, BLOCK_SIDE, BLOCK_SIDE), jnp.float32) * spread
    symmetric = 0.5 * (offdiagonal_noise + jnp.swapaxes(offdiagonal_noise, 1, 2))
    identity = jnp.eye(BLOCK_SIDE, dtype=jnp.float32)
    return symmetric + identity[None, :, :] * diagonal[:, None, :]


def draw_left_root(key, part):
    key = jax.random.fold_in(key, 11)
    return root_matrix(key, 0.5 / math.sqrt(BLOCK_SIDE), 2.0).astype(jnp.bfloat16)


def draw_right_root(key, part):
    key = jax.random.fold_in(key, 23)
    return root_matrix(key, 0.5 / math.sqrt(BLOCK_SIDE), 2.0).astype(jnp.bfloat16)


def steps_of(rng, dims, cuts, smallest, largest):
    gain = 1.0
    for dim, shards_of in cuts:
        heights = jax.random.uniform(jax.random.fold_in(jax.random.fold_in(rng, 6), dim), (shards_of,), jnp.float32, smallest / len(cuts), largest / len(cuts))
        gain = gain * jnp.repeat(jnp.exp(heights), dims[dim] // shards_of).reshape((-1,) + (1,) * (len(dims) - 1 - dim))
    return gain


def centred(rng, shape, width, limit, cuts=(), held_as=jnp.bfloat16):
    drawn = jax.random.normal(rng, shape, jnp.float32) * width
    if len(cuts) > 0:
        drawn = steps_of(rng, shape, cuts, -0.22, 0.18) * drawn
    return jnp.clip(drawn, min=-limit, max=limit).astype(held_as)


def setup_inputs(seed: int = 0) -> dict:
    splits = jax.random.split(jax.random.key(seed), 8)
    gradient = draw_gradient(jax.random.fold_in(splits[7], 71), 0)
    block_group = draw_block_group(jax.random.fold_in(splits[7], 71), 0)
    block_owner = draw_block_owner(jax.random.fold_in(splits[7], 71), 0)
    left_kronecker = centred(splits[3], (SLOT_TOTAL_COUNT, BLOCK_SIDE, BLOCK_SIDE), 1.0, 6.0, ((0, 256),), jnp.float32)
    right_kronecker = centred(splits[4], (SLOT_TOTAL_COUNT, BLOCK_SIDE, BLOCK_SIDE), 1.0, 6.0, ((0, 256),), jnp.float32)
    left_root = draw_left_root(jax.random.fold_in(splits[7], 71), 0)
    right_root = draw_right_root(jax.random.fold_in(splits[7], 71), 0)
    return dict(gradient=gradient, block_group=block_group, block_owner=block_owner, left_kronecker=left_kronecker, right_kronecker=right_kronecker, left_root=left_root, right_root=right_root)


decay_rate = 0.9
epsilon = 1e-06

def reference(gradient, block_group, block_owner, left_kronecker, right_kronecker, left_root, right_root):
    block_count = gradient.shape[0]
    block_ids = jnp.arange(block_count, dtype=jnp.int32)
    earlier_twin = (block_group[:, None] == block_group[None, :]) & (block_owner[:, None] == block_owner[None, :]) & (block_ids[None, :] < block_ids[:, None])
    slot_rank = lax.optimization_barrier(jnp.sum(earlier_twin.astype(jnp.int32), axis=1)).astype(jnp.int32)
    position = ((block_group * N_FSDP + block_owner) * SLOTS + slot_rank).astype(jnp.int32)

    def one_block(block_item):
        block_grad, slot_pos = block_item
        left_gram = jnp.dot(block_grad, block_grad.T, preferred_element_type=jnp.float32)
        right_gram = jnp.dot(block_grad.T, block_grad, preferred_element_type=jnp.float32)
        left_next = decay_rate * left_kronecker[slot_pos] + (1.0 - decay_rate) / BLOCK_SIDE * left_gram
        right_following = decay_rate * right_kronecker[slot_pos] + (1.0 - decay_rate) / BLOCK_SIDE * right_gram
        partial_value = jnp.dot(left_root[slot_pos], block_grad, preferred_element_type=jnp.float32).astype(jnp.bfloat16)
        precond = jnp.dot(partial_value, right_root[slot_pos], preferred_element_type=jnp.float32)
        grad_wide = block_grad.astype(jnp.float32)
        grad_norm = jnp.sqrt(jnp.sum(grad_wide * grad_wide))
        precond_norm = jnp.sqrt(jnp.sum(precond * precond) + epsilon)
        block_update = (precond * (grad_norm / precond_norm)).astype(jnp.bfloat16)
        return (left_next, right_following, block_update)
    left_blocks, right_blocks, update = lax.map(one_block, (gradient, position))
    new_left = (decay_rate * left_kronecker).at[position].set(left_blocks)
    new_right = (decay_rate * right_kronecker).at[position].set(right_blocks)
    return (new_left, new_right, update)
```

```python
import jax
import jax.numpy as jnp
from jax import lax
from jax.experimental import pallas as pl
from jax.experimental.pallas import tpu as pltpu
from jax.sharding import PartitionSpec as P

BLOCK_SIDE = 512
NREP = 4
NZ = 8
NYC = 8
NF = NZ * NYC
ROWS = 8
NBLK = 192

decay_rate = 0.9
epsilon = 1e-06
MESH = pl.DeviceIdType.MESH
DMA = pltpu.SemaphoreType.DMA
bf16 = jnp.bfloat16
f32 = jnp.float32

FAR_FIRST = (4, 3, 5, 2, 6, 1, 7, 0)
NEAR_FIRST = (0, 1, 7, 2, 6, 3, 5, 4)


def step_kernel(
    src_ref, coef_ref, grad_hbm, lk_hbm, rk_hbm, lroot_hbm, rroot_hbm,
    all_ref, nl_ref, nr_ref,
    grad, outgoing, landed, lk, rk, lroot, rroot, upd,
    in_sem, send1, recv1, send2, recv2, sendx, recvx, sendr, recvr,
):
    rep = lax.axis_index("rep")
    me = lax.axis_index("fsdp")
    z = me // NYC
    yc = me % NYC
    right = (rep + 1) % NREP
    left = (rep + NREP - 1) % NREP

    barrier = pltpu.get_barrier_semaphore()

    @pl.loop(1, NF)
    def _(s):
        pl.semaphore_signal(
            barrier, inc=1, device_id={"fsdp": lax.rem(me + s, NF)}, device_id_type=MESH
        )

    for peer in (left, right):
        pl.semaphore_signal(barrier, inc=1, device_id={"rep": peer}, device_id_type=MESH)

    pairs = ((grad_hbm, grad), (lroot_hbm, lroot), (rroot_hbm, rroot), (lk_hbm, lk), (rk_hbm, rk))
    loads = [pltpu.make_async_copy(a, b, in_sem.at[i]) for i, (a, b) in enumerate(pairs)]
    for load in loads:
        load.start()
    loads[0].wait()

    @pl.loop(0, NF)
    def _(o):
        outgoing[o] = grad[src_ref[o]]

    pl.semaphore_wait(barrier, NF + 1)

    for d in FAR_FIRST:
        @pl.loop(0, NYC)
        def _(j):
            target = lax.rem(z + d, NZ) * NYC + lax.rem(yc + j, NYC)

            def go():
                pltpu.make_async_remote_copy(
                    src_ref=outgoing.at[target], dst_ref=landed.at[me],
                    send_sem=send1, recv_sem=recv1,
                    device_id={"fsdp": target}, device_id_type=MESH,
                ).start()

            if d == 0:
                pl.when(j > 0)(go)
            else:
                go()

    landed[me] = outgoing[me]
    loads[1].wait()
    loads[2].wait()
    whole1 = pltpu.make_async_remote_copy(
        src_ref=outgoing.at[pl.ds(0, NF - 1)], dst_ref=landed.at[pl.ds(0, NF - 1)],
        send_sem=send1, recv_sem=recv1, device_id={"fsdp": me}, device_id_type=MESH,
    )
    whole1.wait_recv()

    g = landed[...].reshape(BLOCK_SIDE, BLOCK_SIDE)
    partial = jnp.dot(lroot[0], g, preferred_element_type=f32).astype(bf16)
    precond = jnp.dot(partial, rroot[0], preferred_element_type=f32)
    wide = g.astype(f32)
    grad_norm = jnp.sqrt(jnp.sum(wide * wide, keepdims=True))
    precond_norm = jnp.sqrt(jnp.sum(precond * precond, keepdims=True) + epsilon)
    update = (precond * (grad_norm / precond_norm)).astype(bf16)
    upd[...] = update.reshape(NF, ROWS, BLOCK_SIDE)

    for i, d in enumerate(NEAR_FIRST):
        @pl.loop(0, NYC)
        def _(j):
            target = lax.rem(z + d, NZ) * NYC + lax.rem(yc + j, NYC)

            def go():
                pltpu.make_async_remote_copy(
                    src_ref=upd.at[target], dst_ref=all_ref.at[rep, me],
                    send_sem=send2, recv_sem=recv2.at[i],
                    device_id={"fsdp": target}, device_id_type=MESH,
                ).start()

            if d == 0:
                pl.when(j > 0)(go)
            else:
                go()

    all_ref[rep, me] = upd[me]

    def chunk(group, i):
        source = lax.rem(z + NZ - NEAR_FIRST[i], NZ)
        return all_ref.at[group, pl.ds(source * NYC, NYC)]

    def own(i, way):
        return pltpu.make_async_remote_copy(
            src_ref=chunk(rep, i), dst_ref=chunk(rep, i),
            send_sem=sendx, recv_sem=recvx.at[i, way],
            device_id={"rep": (right, left)[way]}, device_id_type=MESH,
        )

    def relay(i):
        way = i % 2
        group = (left, right)[way]
        return pltpu.make_async_remote_copy(
            src_ref=chunk(group, i), dst_ref=chunk(group, i),
            send_sem=sendr, recv_sem=recvr.at[i],
            device_id={"rep": (right, left)[way]}, device_id_type=MESH,
        )

    def landed_chunk(i):
        n = NYC - 1 if i == 0 else NYC
        return pltpu.make_async_remote_copy(
            src_ref=upd.at[pl.ds(0, n)], dst_ref=all_ref.at[rep, pl.ds(0, n)],
            send_sem=send2, recv_sem=recv2.at[i], device_id={"fsdp": me}, device_id_type=MESH,
        )

    loads[3].wait()
    loads[4].wait()
    coef = coef_ref[0]
    half = BLOCK_SIDE // 2

    def left_piece(k):
        rows = landed[pl.ds(k * NF // 2, NF // 2)].reshape(half, BLOCK_SIDE)
        gram = lax.dot_general(
            rows, landed[...].reshape(BLOCK_SIDE, BLOCK_SIDE), (((1,), (1,)), ((), ())),
            preferred_element_type=f32,
        )
        at = pl.ds(k * half, half)
        nl_ref[0, at, :] = decay_rate * lk[0, at, :] + coef * gram

    def right_piece(k):
        at = pl.ds(k * half, half)
        block = landed[...].reshape(BLOCK_SIDE, BLOCK_SIDE)
        gram = lax.dot_general(
            block[:, k * half:(k + 1) * half], block, (((0,), (0,)), ((), ())),
            preferred_element_type=f32,
        )
        nr_ref[0, at, :] = decay_rate * rk[0, at, :] + coef * gram

    work = {0: lambda: left_piece(0), 1: lambda: left_piece(1), 2: lambda: right_piece(0), 3: lambda: right_piece(1)}
    for i in range(NZ):
        landed_chunk(i).wait_recv()
        own(i, 0).start()
        own(i, 1).start()
        if i in work:
            work[i]()
        if i >= 1:
            own(i - 1, (i - 1) % 2).wait_recv()
            relay(i - 1).start()
    own(NZ - 1, (NZ - 1) % 2).wait_recv()
    relay(NZ - 1).start()
    for i in range(NZ):
        own(i, 1 - i % 2).wait_recv()
        relay(i).wait_recv()

    whole1.wait_send()
    pltpu.make_async_remote_copy(
        src_ref=upd.at[pl.ds(0, NF - 1)], dst_ref=all_ref.at[rep, pl.ds(0, NF - 1)],
        send_sem=send2, recv_sem=recv2.at[0], device_id={"fsdp": me}, device_id_type=MESH,
    ).wait_send()
    for i in range(NZ):
        own(i, 0).wait_send()
        own(i, 1).wait_send()
        relay(i).wait_send()


def finish_kernel(pick_ref, all_ref, nl_ref, nr_ref, out_hbm, nl_hbm, nr_hbm, out, sem):
    copies = [
        pltpu.make_async_copy(nl_ref, nl_hbm, sem.at[0]),
        pltpu.make_async_copy(nr_ref, nr_hbm, sem.at[1]),
    ]
    for c in copies:
        c.start()
    parts = 4
    n = NBLK // parts
    for p in range(parts):
        @pl.loop(p * n, (p + 1) * n, unroll=8)
        def _(b):
            out[b] = all_ref[pick_ref[b]]

        c = pltpu.make_async_copy(
            out.at[pl.ds(p * n, n)], out_hbm.at[pl.ds(p * n, n)], sem.at[2 + p]
        )
        c.start()
        copies.append(c)
    for c in copies:
        c.wait()


def per_device(
    gradient, block_group, block_owner, left_kronecker, right_kronecker, left_root, right_root
):
    my_group = lax.axis_index("rep")
    me = lax.axis_index("fsdp")
    block_ids = jnp.arange(NBLK, dtype=jnp.int32)
    key = block_group * NF + block_owner
    earlier_twin = (key[:, None] == key[None, :]) & (block_ids[None, :] < block_ids[:, None])
    position = key + jnp.sum(earlier_twin.astype(jnp.int32), axis=1)
    wanted = my_group * NF + jnp.arange(NF, dtype=jnp.int32)
    matches = position[None, :] == wanted[:, None]
    source = jnp.sum(jnp.where(matches, block_ids[None, :], 0), axis=1)
    present = jnp.any(position == my_group * NF + me)
    coef = jnp.where(present, (1.0 - decay_rate) / BLOCK_SIDE, 0.0).astype(f32).reshape(1)

    vmem = pl.BlockSpec(memory_space=pltpu.VMEM)
    smem = pl.BlockSpec(memory_space=pltpu.SMEM)
    anyspace = pl.BlockSpec(memory_space=pl.ANY)
    strips = (NF, ROWS, BLOCK_SIDE)
    square = (1, BLOCK_SIDE, BLOCK_SIDE)
    everything, nl, nr = pl.pallas_call(
        step_kernel,
        out_shape=(
            jax.ShapeDtypeStruct((NREP,) + strips, bf16),
            jax.ShapeDtypeStruct(square, f32),
            jax.ShapeDtypeStruct(square, f32),
        ),
        in_specs=[smem, smem] + [anyspace] * 5,
        out_specs=(vmem,) * 3,
        scratch_shapes=[
            pltpu.VMEM((NBLK, ROWS, BLOCK_SIDE), bf16),
            pltpu.VMEM(strips, bf16),
            pltpu.VMEM(strips, bf16),
            pltpu.VMEM(square, f32),
            pltpu.VMEM(square, f32),
            pltpu.VMEM(square, bf16),
            pltpu.VMEM(square, bf16),
            pltpu.VMEM(strips, bf16),
            DMA((5,)),
            DMA, DMA,
            DMA, DMA((NZ,)),
            DMA, DMA((NZ, 2)),
            DMA, DMA((NZ,)),
        ],
        name="shampoo_step",
        cost_estimate=pl.CostEstimate(
            flops=8 * BLOCK_SIDE**3, bytes_accessed=8 << 20, transcendentals=0
        ),
        compiler_params=pltpu.CompilerParams(
            collective_id=0, has_side_effects=True, vmem_limit_bytes=56 << 20
        ),
    )(source, coef, gradient, left_kronecker, right_kronecker, left_root, right_root)
    update, new_left, new_right = pl.pallas_call(
        finish_kernel,
        out_shape=(
            jax.ShapeDtypeStruct((NBLK, ROWS, BLOCK_SIDE), bf16),
            jax.ShapeDtypeStruct(square, f32),
            jax.ShapeDtypeStruct(square, f32),
        ),
        in_specs=[smem, vmem, vmem, vmem],
        out_specs=(anyspace,) * 3,
        scratch_shapes=[pltpu.VMEM((NBLK, ROWS, BLOCK_SIDE), bf16), DMA((6,))],
        name="place_update",
        compiler_params=pltpu.CompilerParams(vmem_limit_bytes=40 << 20),
    )(position, everything.reshape(NREP * NF, ROWS, BLOCK_SIDE), nl, nr)
    return (new_left, new_right, update)


def solution(mesh):
    in_specs = (
        P(None, "fsdp", None),
        P(),
        P(),
        P(("rep", "fsdp"), None, None),
        P(("rep", "fsdp"), None, None),
        P(("rep", "fsdp"), None, None),
        P(("rep", "fsdp"), None, None),
    )
    out_specs = (
        P(("rep", "fsdp"), None, None),
        P(("rep", "fsdp"), None, None),
        P(None, "fsdp", None),
    )
    return jax.shard_map(
        per_device, mesh=mesh, in_specs=in_specs, out_specs=out_specs, check_vma=False
    )
```

```python
import jax
import jax.numpy as jnp
from jax import lax
from jax.experimental import pallas as pl
from jax.experimental.pallas import tpu as pltpu
from jax.sharding import PartitionSpec as P

BLOCK_SIDE = 512
NREP = 4
NZ = 8
NYC = 8
NF = NZ * NYC
ROWS = 8
NBLK = 192

decay_rate = 0.9
epsilon = 1e-06
MESH = pl.DeviceIdType.MESH
DMA = pltpu.SemaphoreType.DMA
bf16 = jnp.bfloat16
f32 = jnp.float32

FAR_FIRST = (4, 3, 5, 2, 6, 1, 7, 0)
NEAR_FIRST = (0, 1, 7, 2, 6, 3, 5, 4)


def step_kernel(
    src_ref, coef_ref, grad_hbm, lk_hbm, rk_hbm, lroot_hbm, rroot_hbm,
    all_ref, nl_ref, nr_ref,
    grad, outgoing, landed, lk, rk, lroot, rroot, upd,
    in_sem, send1, recv1, send2, recv2, sendx, recvx, sendr, recvr,
):
    rep = lax.axis_index("rep")
    me = lax.axis_index("fsdp")
    z = me // NYC
    yc = me % NYC
    right = (rep + 1) % NREP
    left = (rep + NREP - 1) % NREP

    barrier = pltpu.get_barrier_semaphore()

    @pl.loop(1, NF)
    def _(s):
        pl.semaphore_signal(
            barrier, inc=1, device_id={"fsdp": lax.rem(me + s, NF)}, device_id_type=MESH
        )

    for peer in (left, right):
        pl.semaphore_signal(barrier, inc=1, device_id={"rep": peer}, device_id_type=MESH)

    pairs = ((grad_hbm, grad), (lroot_hbm, lroot), (rroot_hbm, rroot), (lk_hbm, lk), (rk_hbm, rk))
    loads = [pltpu.make_async_copy(a, b, in_sem.at[i]) for i, (a, b) in enumerate(pairs)]
    for load in loads:
        load.start()
    loads[0].wait()

    @pl.loop(0, NF)
    def _(o):
        outgoing[o] = grad[src_ref[o]]

    pl.semaphore_wait(barrier, NF + 1)

    for d in FAR_FIRST:
        @pl.loop(0, NYC)
        def _(j):
            target = lax.rem(z + d, NZ) * NYC + lax.rem(yc + j, NYC)

            def go():
                pltpu.make_async_remote_copy(
                    src_ref=outgoing.at[target], dst_ref=landed.at[me],
                    send_sem=send1, recv_sem=recv1,
                    device_id={"fsdp": target}, device_id_type=MESH,
                ).start()

            if d == 0:
                pl.when(j > 0)(go)
            else:
                go()

    landed[me] = outgoing[me]
    loads[1].wait()
    loads[2].wait()
    whole1 = pltpu.make_async_remote_copy(
        src_ref=outgoing.at[pl.ds(0, NF - 1)], dst_ref=landed.at[pl.ds(0, NF - 1)],
        send_sem=send1, recv_sem=recv1, device_id={"fsdp": me}, device_id_type=MESH,
    )
    whole1.wait_recv()

    g = landed[...].reshape(BLOCK_SIDE, BLOCK_SIDE)
    partial = jnp.dot(lroot[0], g, preferred_element_type=f32).astype(bf16)
    precond = jnp.dot(partial, rroot[0], preferred_element_type=f32)
    wide = g.astype(f32)
    grad_norm = jnp.sqrt(jnp.sum(wide * wide, keepdims=True))
    precond_norm = jnp.sqrt(jnp.sum(precond * precond, keepdims=True) + epsilon)
    update = (precond * (grad_norm / precond_norm)).astype(bf16)
    upd[...] = update.reshape(NF, ROWS, BLOCK_SIDE)

    for i, d in enumerate(NEAR_FIRST):
        @pl.loop(0, NYC)
        def _(j):
            target = lax.rem(z + d, NZ) * NYC + lax.rem(yc + j, NYC)

            def go():
                pltpu.make_async_remote_copy(
                    src_ref=upd.at[target], dst_ref=all_ref.at[rep, me],
                    send_sem=send2, recv_sem=recv2.at[i],
                    device_id={"fsdp": target}, device_id_type=MESH,
                ).start()

            if d == 0:
                pl.when(j > 0)(go)
            else:
                go()

    all_ref[rep, me] = upd[me]

    def chunk(group, i):
        source = lax.rem(z + NZ - NEAR_FIRST[i], NZ)
        return all_ref.at[group, pl.ds(source * NYC, NYC)]

    def own(i, way):
        return pltpu.make_async_remote_copy(
            src_ref=chunk(rep, i), dst_ref=chunk(rep, i),
            send_sem=sendx, recv_sem=recvx.at[i, way],
            device_id={"rep": (right, left)[way]}, device_id_type=MESH,
        )

    def relay(i):
        way = i % 2
        group = (left, right)[way]
        return pltpu.make_async_remote_copy(
            src_ref=chunk(group, i), dst_ref=chunk(group, i),
            send_sem=sendr, recv_sem=recvr.at[i],
            device_id={"rep": (right, left)[way]}, device_id_type=MESH,
        )

    def landed_chunk(i):
        n = NYC - 1 if i == 0 else NYC
        return pltpu.make_async_remote_copy(
            src_ref=upd.at[pl.ds(0, n)], dst_ref=all_ref.at[rep, pl.ds(0, n)],
            send_sem=send2, recv_sem=recv2.at[i], device_id={"fsdp": me}, device_id_type=MESH,
        )

    loads[3].wait()
    loads[4].wait()
    coef = coef_ref[0]
    half = BLOCK_SIDE // 2

    def left_piece(k):
        rows = landed[pl.ds(k * NF // 2, NF // 2)].reshape(half, BLOCK_SIDE)
        gram = lax.dot_general(
            rows, landed[...].reshape(BLOCK_SIDE, BLOCK_SIDE), (((1,), (1,)), ((), ())),
            preferred_element_type=f32,
        )
        at = pl.ds(k * half, half)
        nl_ref[0, at, :] = decay_rate * lk[0, at, :] + coef * gram

    def right_piece(k):
        at = pl.ds(k * half, half)
        block = landed[...].reshape(BLOCK_SIDE, BLOCK_SIDE)
        gram = lax.dot_general(
            block[:, k * half:(k + 1) * half], block, (((0,), (0,)), ((), ())),
            preferred_element_type=f32,
        )
        nr_ref[0, at, :] = decay_rate * rk[0, at, :] + coef * gram

    work = {0: lambda: left_piece(0), 1: lambda: left_piece(1), 2: lambda: right_piece(0), 3: lambda: right_piece(1)}
    for i in range(NZ):
        landed_chunk(i).wait_recv()
        own(i, 0).start()
        own(i, 1).start()
        if i in work:
            work[i]()
        if i >= 1:
            own(i - 1, (i - 1) % 2).wait_recv()
            relay(i - 1).start()
    own(NZ - 1, (NZ - 1) % 2).wait_recv()
    relay(NZ - 1).start()
    for i in range(NZ):
        own(i, 1 - i % 2).wait_recv()
        relay(i).wait_recv()

    whole1.wait_send()
    pltpu.make_async_remote_copy(
        src_ref=upd.at[pl.ds(0, NF - 1)], dst_ref=all_ref.at[rep, pl.ds(0, NF - 1)],
        send_sem=send2, recv_sem=recv2.at[0], device_id={"fsdp": me}, device_id_type=MESH,
    ).wait_send()
    for i in range(NZ):
        own(i, 0).wait_send()
        own(i, 1).wait_send()
        relay(i).wait_send()


def finish_kernel(pick_ref, all_ref, nl_ref, nr_ref, out_hbm, nl_hbm, nr_hbm, out, sem):
    copies = [
        pltpu.make_async_copy(nl_ref, nl_hbm, sem.at[0]),
        pltpu.make_async_copy(nr_ref, nr_hbm, sem.at[1]),
    ]
    for c in copies:
        c.start()
    parts = 4
    n = NBLK // parts
    for p in range(parts):
        @pl.loop(p * n, (p + 1) * n, unroll=8)
        def _(b):
            out[b] = all_ref[pick_ref[b]]

        c = pltpu.make_async_copy(
            out.at[pl.ds(p * n, n)], out_hbm.at[pl.ds(p * n, n)], sem.at[2 + p]
        )
        c.start()
        copies.append(c)
    for c in copies:
        c.wait()


def per_device(
    gradient, block_group, block_owner, left_kronecker, right_kronecker, left_root, right_root
):
    my_group = lax.axis_index("rep")
    me = lax.axis_index("fsdp")
    block_ids = jnp.arange(NBLK, dtype=jnp.int32)
    key = block_group * NF + block_owner
    earlier_twin = (key[:, None] == key[None, :]) & (block_ids[None, :] < block_ids[:, None])
    position = key + jnp.sum(earlier_twin.astype(jnp.int32), axis=1)
    wanted = my_group * NF + jnp.arange(NF, dtype=jnp.int32)
    matches = position[None, :] == wanted[:, None]
    source = jnp.sum(jnp.where(matches, block_ids[None, :], 0), axis=1)
    present = jnp.any(position == my_group * NF + me)
    coef = jnp.where(present, (1.0 - decay_rate) / BLOCK_SIDE, 0.0).astype(f32).reshape(1)

    vmem = pl.BlockSpec(memory_space=pltpu.VMEM)
    smem = pl.BlockSpec(memory_space=pltpu.SMEM)
    anyspace = pl.BlockSpec(memory_space=pl.ANY)
    strips = (NF, ROWS, BLOCK_SIDE)
    square = (1, BLOCK_SIDE, BLOCK_SIDE)
    everything, nl, nr = pl.pallas_call(
        step_kernel,
        out_shape=(
            jax.ShapeDtypeStruct((NREP,) + strips, bf16),
            jax.ShapeDtypeStruct(square, f32),
            jax.ShapeDtypeStruct(square, f32),
        ),
        in_specs=[smem, smem] + [anyspace] * 5,
        out_specs=(vmem,) * 3,
        scratch_shapes=[
            pltpu.VMEM((NBLK, ROWS, BLOCK_SIDE), bf16),
            pltpu.VMEM(strips, bf16),
            pltpu.VMEM(strips, bf16),
            pltpu.VMEM(square, f32),
            pltpu.VMEM(square, f32),
            pltpu.VMEM(square, bf16),
            pltpu.VMEM(square, bf16),
            pltpu.VMEM(strips, bf16),
            DMA((5,)),
            DMA, DMA,
            DMA, DMA((NZ,)),
            DMA, DMA((NZ, 2)),
            DMA, DMA((NZ,)),
        ],
        name="shampoo_step",
        cost_estimate=pl.CostEstimate(
            flops=8 * BLOCK_SIDE**3, bytes_accessed=8 << 20, transcendentals=0
        ),
        compiler_params=pltpu.CompilerParams(
            collective_id=0, has_side_effects=True, vmem_limit_bytes=32 << 20
        ),
    )(source, coef, *[pltpu.with_memory_space_constraint(x, pltpu.HBM) for x in (gradient, left_kronecker, right_kronecker, left_root, right_root)])
    update, new_left, new_right = pl.pallas_call(
        finish_kernel,
        out_shape=(
            jax.ShapeDtypeStruct((NBLK, ROWS, BLOCK_SIDE), bf16),
            jax.ShapeDtypeStruct(square, f32),
            jax.ShapeDtypeStruct(square, f32),
        ),
        in_specs=[smem, vmem, vmem, vmem],
        out_specs=(anyspace,) * 3,
        scratch_shapes=[pltpu.VMEM((NBLK, ROWS, BLOCK_SIDE), bf16), DMA((6,))],
        name="place_update",
        compiler_params=pltpu.CompilerParams(vmem_limit_bytes=40 << 20),
    )(position, everything.reshape(NREP * NF, ROWS, BLOCK_SIDE), nl, nr)
    return (new_left, new_right, update)


def solution(mesh):
    in_specs = (
        P(None, "fsdp", None),
        P(),
        P(),
        P(("rep", "fsdp"), None, None),
        P(("rep", "fsdp"), None, None),
        P(("rep", "fsdp"), None, None),
        P(("rep", "fsdp"), None, None),
    )
    out_specs = (
        P(("rep", "fsdp"), None, None),
        P(("rep", "fsdp"), None, None),
        P(None, "fsdp", None),
    )
    return jax.shard_map(
        per_device, mesh=mesh, in_specs=in_specs, out_specs=out_specs, check_vma=False
    )
```

```python
import jax
import jax.numpy as jnp
from jax import lax
from jax.experimental import pallas as pl
from jax.experimental.pallas import tpu as pltpu
from jax.sharding import PartitionSpec as P

BLOCK_SIDE = 512
NREP = 4
NZ = 8
NYC = 8
NF = NZ * NYC
ROWS = 8
NBLK = 192

decay_rate = 0.9
epsilon = 1e-06
MESH = pl.DeviceIdType.MESH
DMA = pltpu.SemaphoreType.DMA
bf16 = jnp.bfloat16
f32 = jnp.float32

FAR_FIRST = (4, 3, 5, 2, 6, 1, 7, 0)
NEAR_FIRST = (0, 1, 7, 2, 6, 3, 5, 4)


def step_kernel(
    group_hbm, owner_hbm, grad_hbm, lk_hbm, rk_hbm, lroot_hbm, rroot_hbm,
    all_ref, nl_ref, nr_ref, pos_ref,
    group, owner, source_row, source,
    grad, outgoing, landed, lk, rk, lroot, rroot, upd,
    in_sem, send1, recv1, send2, recv2, sendx, recvx, sendr, recvr,
):
    rep = lax.axis_index("rep")
    me = lax.axis_index("fsdp")
    z = me // NYC
    yc = me % NYC
    right = (rep + 1) % NREP
    left = (rep + NREP - 1) % NREP

    barrier = pltpu.get_barrier_semaphore()

    @pl.loop(1, NF)
    def _(s):
        pl.semaphore_signal(
            barrier, inc=1, device_id={"fsdp": lax.rem(me + s, NF)}, device_id_type=MESH
        )

    for peer in (left, right):
        pl.semaphore_signal(barrier, inc=1, device_id={"rep": peer}, device_id_type=MESH)

    pairs = (
        (group_hbm, group), (owner_hbm, owner), (grad_hbm, grad),
        (lroot_hbm, lroot), (rroot_hbm, rroot), (lk_hbm, lk), (rk_hbm, rk),
    )
    loads = [pltpu.make_async_copy(a, b, in_sem.at[i]) for i, (a, b) in enumerate(pairs)]
    for load in loads:
        load.start()
    loads[0].wait()
    loads[1].wait()

    key = group[...] * NF + owner[...]
    c = lax.broadcasted_iota(jnp.int32, (NBLK, NBLK), 0)
    b = lax.broadcasted_iota(jnp.int32, (NBLK, NBLK), 1)
    key_column = jnp.sum(jnp.where(b == c, key, 0), axis=1, keepdims=True)
    rank = jnp.sum(jnp.where((key_column == key) & (c < b), 1, 0), axis=0, keepdims=True)
    position = key + rank
    pos_ref[...] = position
    slot = lax.broadcasted_iota(jnp.int32, (NF, NBLK), 0)
    block = lax.broadcasted_iota(jnp.int32, (NF, NBLK), 1)
    match = position == slot + rep * NF
    source_column = jnp.sum(jnp.where(match, block, 0), axis=1, keepdims=True)
    down = lax.broadcasted_iota(jnp.int32, (NF, 128), 0)
    across = lax.broadcasted_iota(jnp.int32, (NF, 128), 1)
    source_row[...] = jnp.sum(jnp.where(down == across, source_column, 0), axis=0, keepdims=True)
    to_scalars = pltpu.make_async_copy(source_row, source, in_sem.at[7])
    to_scalars.start()
    present = jnp.sum(jnp.where(position == rep * NF + me, 1, 0), axis=1, keepdims=True)
    coef = jnp.where(present > 0, (1.0 - decay_rate) / BLOCK_SIDE, 0.0).astype(f32)
    to_scalars.wait()
    loads[2].wait()

    @pl.loop(0, NF, unroll=8)
    def _(o):
        outgoing[o] = grad[source[0, o]]

    pl.semaphore_wait(barrier, NF + 1)

    for d in FAR_FIRST:
        @pl.loop(0, NYC)
        def _(j):
            target = lax.rem(z + d, NZ) * NYC + lax.rem(yc + j, NYC)

            def go():
                pltpu.make_async_remote_copy(
                    src_ref=outgoing.at[target], dst_ref=landed.at[me],
                    send_sem=send1, recv_sem=recv1,
                    device_id={"fsdp": target}, device_id_type=MESH,
                ).start()

            if d == 0:
                pl.when(j > 0)(go)
            else:
                go()

    landed[me] = outgoing[me]
    loads[3].wait()
    loads[4].wait()
    whole1 = pltpu.make_async_remote_copy(
        src_ref=outgoing.at[pl.ds(0, NF - 1)], dst_ref=landed.at[pl.ds(0, NF - 1)],
        send_sem=send1, recv_sem=recv1, device_id={"fsdp": me}, device_id_type=MESH,
    )
    whole1.wait_recv()

    g = landed[...].reshape(BLOCK_SIDE, BLOCK_SIDE)
    partial = jnp.dot(lroot[0], g, preferred_element_type=f32).astype(bf16)
    precond = jnp.dot(partial, rroot[0], preferred_element_type=f32)
    wide = g.astype(f32)
    grad_norm = jnp.sqrt(jnp.sum(wide * wide, keepdims=True))
    precond_norm = jnp.sqrt(jnp.sum(precond * precond, keepdims=True) + epsilon)
    update = (precond * (grad_norm / precond_norm)).astype(bf16)
    upd[...] = update.reshape(NF, ROWS, BLOCK_SIDE)

    for i, d in enumerate(NEAR_FIRST):
        @pl.loop(0, NYC)
        def _(j):
            target = lax.rem(z + d, NZ) * NYC + lax.rem(yc + j, NYC)

            def go():
                pltpu.make_async_remote_copy(
                    src_ref=upd.at[target], dst_ref=all_ref.at[rep, me],
                    send_sem=send2, recv_sem=recv2.at[i],
                    device_id={"fsdp": target}, device_id_type=MESH,
                ).start()

            if d == 0:
                pl.when(j > 0)(go)
            else:
                go()

    all_ref[rep, me] = upd[me]

    def chunk(group, i):
        source = lax.rem(z + NZ - NEAR_FIRST[i], NZ)
        return all_ref.at[group, pl.ds(source * NYC, NYC)]

    def own(i, way):
        return pltpu.make_async_remote_copy(
            src_ref=chunk(rep, i), dst_ref=chunk(rep, i),
            send_sem=sendx, recv_sem=recvx.at[i, way],
            device_id={"rep": (right, left)[way]}, device_id_type=MESH,
        )

    def relay(i):
        way = i % 2
        group = (left, right)[way]
        return pltpu.make_async_remote_copy(
            src_ref=chunk(group, i), dst_ref=chunk(group, i),
            send_sem=sendr, recv_sem=recvr.at[i],
            device_id={"rep": (right, left)[way]}, device_id_type=MESH,
        )

    def landed_chunk(i):
        n = NYC - 1 if i == 0 else NYC
        return pltpu.make_async_remote_copy(
            src_ref=upd.at[pl.ds(0, n)], dst_ref=all_ref.at[rep, pl.ds(0, n)],
            send_sem=send2, recv_sem=recv2.at[i], device_id={"fsdp": me}, device_id_type=MESH,
        )

    loads[5].wait()
    loads[6].wait()
    half = BLOCK_SIDE // 2

    def left_piece(k):
        rows = landed[pl.ds(k * NF // 2, NF // 2)].reshape(half, BLOCK_SIDE)
        gram = lax.dot_general(
            rows, landed[...].reshape(BLOCK_SIDE, BLOCK_SIDE), (((1,), (1,)), ((), ())),
            preferred_element_type=f32,
        )
        at = pl.ds(k * half, half)
        nl_ref[0, at, :] = decay_rate * lk[0, at, :] + coef * gram

    def right_piece(k):
        at = pl.ds(k * half, half)
        block = landed[...].reshape(BLOCK_SIDE, BLOCK_SIDE)
        gram = lax.dot_general(
            block[:, k * half:(k + 1) * half], block, (((0,), (0,)), ((), ())),
            preferred_element_type=f32,
        )
        nr_ref[0, at, :] = decay_rate * rk[0, at, :] + coef * gram

    work = {0: lambda: left_piece(0), 1: lambda: left_piece(1), 2: lambda: right_piece(0), 3: lambda: right_piece(1)}
    for i in range(NZ):
        landed_chunk(i).wait_recv()
        own(i, 0).start()
        own(i, 1).start()
        if i in work:
            work[i]()
        if i >= 1:
            own(i - 1, (i - 1) % 2).wait_recv()
            relay(i - 1).start()
    own(NZ - 1, (NZ - 1) % 2).wait_recv()
    relay(NZ - 1).start()
    for i in range(NZ):
        own(i, 1 - i % 2).wait_recv()
        relay(i).wait_recv()

    whole1.wait_send()
    pltpu.make_async_remote_copy(
        src_ref=upd.at[pl.ds(0, NF - 1)], dst_ref=all_ref.at[rep, pl.ds(0, NF - 1)],
        send_sem=send2, recv_sem=recv2.at[0], device_id={"fsdp": me}, device_id_type=MESH,
    ).wait_send()
    for i in range(NZ):
        own(i, 0).wait_send()
        own(i, 1).wait_send()
        relay(i).wait_send()


def finish_kernel(pos_ref, all_ref, nl_ref, nr_ref, out_hbm, nl_hbm, nr_hbm, out, pick, sem):
    to_scalars = pltpu.make_async_copy(pos_ref, pick, sem.at[6])
    to_scalars.start()
    copies = [
        pltpu.make_async_copy(nl_ref, nl_hbm, sem.at[0]),
        pltpu.make_async_copy(nr_ref, nr_hbm, sem.at[1]),
    ]
    for c in copies:
        c.start()
    to_scalars.wait()
    parts = 4
    n = NBLK // parts
    for p in range(parts):
        @pl.loop(p * n, (p + 1) * n, unroll=8)
        def _(b):
            out[b] = all_ref[pick[0, b]]

        c = pltpu.make_async_copy(
            out.at[pl.ds(p * n, n)], out_hbm.at[pl.ds(p * n, n)], sem.at[2 + p]
        )
        c.start()
        copies.append(c)
    for c in copies:
        c.wait()


def per_device(
    gradient, block_group, block_owner, left_kronecker, right_kronecker, left_root, right_root
):
    vmem = pl.BlockSpec(memory_space=pltpu.VMEM)
    anyspace = pl.BlockSpec(memory_space=pl.ANY)
    strips = (NF, ROWS, BLOCK_SIDE)
    square = (1, BLOCK_SIDE, BLOCK_SIDE)
    everything, nl, nr, position = pl.pallas_call(
        step_kernel,
        out_shape=(
            jax.ShapeDtypeStruct((NREP,) + strips, bf16),
            jax.ShapeDtypeStruct(square, f32),
            jax.ShapeDtypeStruct(square, f32),
            jax.ShapeDtypeStruct((1, NBLK), jnp.int32),
        ),
        in_specs=[anyspace] * 7,
        out_specs=(vmem,) * 4,
        scratch_shapes=[
            pltpu.VMEM((1, NBLK), jnp.int32),
            pltpu.VMEM((1, NBLK), jnp.int32),
            pltpu.VMEM((1, 128), jnp.int32),
            pltpu.SMEM((1, 128), jnp.int32),
            pltpu.VMEM((NBLK, ROWS, BLOCK_SIDE), bf16),
            pltpu.VMEM(strips, bf16),
            pltpu.VMEM(strips, bf16),
            pltpu.VMEM(square, f32),
            pltpu.VMEM(square, f32),
            pltpu.VMEM(square, bf16),
            pltpu.VMEM(square, bf16),
            pltpu.VMEM(strips, bf16),
            DMA((8,)),
            DMA, DMA,
            DMA, DMA((NZ,)),
            DMA, DMA((NZ, 2)),
            DMA, DMA((NZ,)),
        ],
        name="shampoo_step",
        cost_estimate=pl.CostEstimate(
            flops=8 * BLOCK_SIDE**3, bytes_accessed=8 << 20, transcendentals=0
        ),
        compiler_params=pltpu.CompilerParams(
            collective_id=0, has_side_effects=True, vmem_limit_bytes=32 << 20
        ),
    )(*[
        pltpu.with_memory_space_constraint(x, pltpu.HBM)
        for x in (
            block_group.reshape(1, NBLK), block_owner.reshape(1, NBLK), gradient,
            left_kronecker, right_kronecker, left_root, right_root,
        )
    ])
    update, new_left, new_right = pl.pallas_call(
        finish_kernel,
        out_shape=(
            jax.ShapeDtypeStruct((NBLK, ROWS, BLOCK_SIDE), bf16),
            jax.ShapeDtypeStruct(square, f32),
            jax.ShapeDtypeStruct(square, f32),
        ),
        in_specs=[vmem] * 4,
        out_specs=(anyspace,) * 3,
        scratch_shapes=[
            pltpu.VMEM((NBLK, ROWS, BLOCK_SIDE), bf16),
            pltpu.SMEM((1, NBLK), jnp.int32),
            DMA((7,)),
        ],
        name="place_update",
        compiler_params=pltpu.CompilerParams(vmem_limit_bytes=40 << 20),
    )(position, everything.reshape(NREP * NF, ROWS, BLOCK_SIDE), nl, nr)
    return (new_left, new_right, update)


def solution(mesh):
    in_specs = (
        P(None, "fsdp", None),
        P(),
        P(),
        P(("rep", "fsdp"), None, None),
        P(("rep", "fsdp"), None, None),
        P(("rep", "fsdp"), None, None),
        P(("rep", "fsdp"), None, None),
    )
    out_specs = (
        P(("rep", "fsdp"), None, None),
        P(("rep", "fsdp"), None, None),
        P(None, "fsdp", None),
    )
    return jax.shard_map(
        per_device, mesh=mesh, in_specs=in_specs, out_specs=out_specs, check_vma=False
    )
```

```python
import jax
import jax.numpy as jnp
from jax import lax
from jax.experimental import pallas as pl
from jax.experimental.pallas import tpu as pltpu
from jax.sharding import PartitionSpec as P

BLOCK_SIDE = 512
NREP = 4
NZ = 8
NYC = 8
NF = NZ * NYC
ROWS = 8
NBLK = 192

decay_rate = 0.9
epsilon = 1e-06
MESH = pl.DeviceIdType.MESH
DMA = pltpu.SemaphoreType.DMA
bf16 = jnp.bfloat16
f32 = jnp.float32

FIRST_ORDER = (4, 3, 5, 2, 6, 1, 7, 0)
OVER_FIRST = (0, 1, 7)
ROUND_FIRST = (2, 6, 3, 5, 4)
SPREAD_OWN_FIRST = False
OPPOSITE_AT = 3
WORK_AT = (-1, -1, 0, 1)


def step_kernel(
    group_hbm, owner_hbm, grad_hbm, lk_hbm, rk_hbm, lroot_hbm, rroot_hbm,
    all_ref, nl_ref, nr_ref, pos_ref,
    group, owner, source_row, source,
    grad, outgoing, landed, lk, rk, lroot, rroot, upd,
    in_sem, send1, recv1, send2, recv2, sendx, recvx, sendr, recvr,
    crossed, send_o, recv_o, send_or, recv_or, send_s, recv_s,
):
    rep = lax.axis_index("rep")
    me = lax.axis_index("fsdp")
    z = me // NYC
    yc = me % NYC
    right = (rep + 1) % NREP
    left = (rep + NREP - 1) % NREP

    barrier = pltpu.get_barrier_semaphore()

    @pl.loop(1, NF)
    def _(s):
        pl.semaphore_signal(
            barrier, inc=1, device_id={"fsdp": lax.rem(me + s, NF)}, device_id_type=MESH
        )

    for peer in (left, right):
        pl.semaphore_signal(barrier, inc=1, device_id={"rep": peer}, device_id_type=MESH)

    pairs = (
        (group_hbm, group), (owner_hbm, owner), (grad_hbm, grad),
        (lroot_hbm, lroot), (rroot_hbm, rroot), (lk_hbm, lk), (rk_hbm, rk),
    )
    loads = [pltpu.make_async_copy(a, b, in_sem.at[i]) for i, (a, b) in enumerate(pairs)]
    for load in loads:
        load.start()
    loads[0].wait()
    loads[1].wait()

    key = group[...] * NF + owner[...]
    c = lax.broadcasted_iota(jnp.int32, (NBLK, NBLK), 0)
    b = lax.broadcasted_iota(jnp.int32, (NBLK, NBLK), 1)
    key_column = jnp.sum(jnp.where(b == c, key, 0), axis=1, keepdims=True)
    rank = jnp.sum(jnp.where((key_column == key) & (c < b), 1, 0), axis=0, keepdims=True)
    position = key + rank
    pos_ref[...] = position
    slot = lax.broadcasted_iota(jnp.int32, (NF, NBLK), 0)
    block = lax.broadcasted_iota(jnp.int32, (NF, NBLK), 1)
    match = position == slot + rep * NF
    source_column = jnp.sum(jnp.where(match, block, 0), axis=1, keepdims=True)
    down = lax.broadcasted_iota(jnp.int32, (NF, 128), 0)
    across = lax.broadcasted_iota(jnp.int32, (NF, 128), 1)
    source_row[...] = jnp.sum(jnp.where(down == across, source_column, 0), axis=0, keepdims=True)
    to_scalars = pltpu.make_async_copy(source_row, source, in_sem.at[7])
    to_scalars.start()
    present = jnp.sum(jnp.where(position == rep * NF + me, 1, 0), axis=1, keepdims=True)
    coef = jnp.where(present > 0, (1.0 - decay_rate) / BLOCK_SIDE, 0.0).astype(f32)
    to_scalars.wait()
    loads[2].wait()

    @pl.loop(0, NF, unroll=8)
    def _(o):
        outgoing[o] = grad[source[0, o]]

    pl.semaphore_wait(barrier, NF + 1)

    @pl.loop(0, NYC)
    def _(j):
        for d in FIRST_ORDER:
            target = lax.rem(z + d, NZ) * NYC + lax.rem(yc + j, NYC)

            def go():
                pltpu.make_async_remote_copy(
                    src_ref=outgoing.at[target], dst_ref=landed.at[me],
                    send_sem=send1, recv_sem=recv1,
                    device_id={"fsdp": target}, device_id_type=MESH,
                ).start()

            if d == 0:
                pl.when(j > 0)(go)
            else:
                go()

    landed[me] = outgoing[me]
    loads[3].wait()
    loads[4].wait()
    whole1 = pltpu.make_async_remote_copy(
        src_ref=outgoing.at[pl.ds(0, NF - 1)], dst_ref=landed.at[pl.ds(0, NF - 1)],
        send_sem=send1, recv_sem=recv1, device_id={"fsdp": me}, device_id_type=MESH,
    )
    whole1.wait_recv()

    g = landed[...].reshape(BLOCK_SIDE, BLOCK_SIDE)
    partial = jnp.dot(lroot[0], g, preferred_element_type=f32).astype(bf16)
    precond = jnp.dot(partial, rroot[0], preferred_element_type=f32)
    wide = g.astype(f32)
    grad_norm = jnp.sqrt(jnp.sum(wide * wide, keepdims=True))
    precond_norm = jnp.sqrt(jnp.sum(precond * precond, keepdims=True) + epsilon)
    update = (precond * (grad_norm / precond_norm)).astype(bf16)
    upd[...] = update.reshape(NF, ROWS, BLOCK_SIDE)

    def remote(src, dst, send, recv, device):
        return pltpu.make_async_remote_copy(
            src_ref=src, dst_ref=dst, send_sem=send, recv_sem=recv,
            device_id=device, device_id_type=MESH,
        )

    ways = ({"rep": right}, {"rep": left})
    came_from = (left, right)
    opposite = (rep + 2) % NREP

    def plane_of(d):
        return lax.rem(z + d, NZ)

    def over(k, way):
        return remote(
            upd.at[pl.ds(plane_of(OVER_FIRST[k]) * NYC, NYC)], crossed.at[rep, k],
            send_o, recv_o.at[k, way], ways[way],
        )

    def over_relay(k, way):
        part = crossed.at[came_from[way], k, pl.ds(way * (NYC // 2), NYC // 2)]
        return remote(part, part, send_or, recv_or.at[k, way], ways[way])

    def spread(k, group, strip):
        d = OVER_FIRST[k]

        @pl.loop(0, NYC)
        def _(j):
            t = lax.rem(yc + j, NYC)

            def go():
                remote(
                    strip(t), all_ref.at[group, me], send_s, recv_s,
                    {"fsdp": plane_of(d) * NYC + t},
                ).start()

            if d == 0:
                pl.when(j > 0)(go)
            else:
                go()

        if d == 0:
            all_ref[group, me] = strip(yc)[...]

    def spread_own():
        for k in range(len(OVER_FIRST)):
            spread(k, rep, lambda t: upd.at[plane_of(OVER_FIRST[k]) * NYC + t])

    for k in range(len(OVER_FIRST)):
        over(k, 0).start()
        over(k, 1).start()

    if SPREAD_OWN_FIRST:
        spread_own()

    for i, d in enumerate(ROUND_FIRST):
        @pl.loop(0, NYC)
        def _(j):
            target = plane_of(d) * NYC + lax.rem(yc + j, NYC)

            def go():
                remote(
                    upd.at[target], all_ref.at[rep, me], send2, recv2.at[i], {"fsdp": target}
                ).start()

            if d == 0:
                pl.when(j > 0)(go)
            else:
                go()

        if d == 0:
            all_ref[rep, me] = upd[me]

    if not SPREAD_OWN_FIRST:
        spread_own()

    def chunk(group, i):
        return all_ref.at[group, pl.ds(plane_of(NZ - ROUND_FIRST[i]) * NYC, NYC)]

    def own(i, way):
        return remote(chunk(rep, i), chunk(rep, i), sendx, recvx.at[i, way], ways[way])

    def relay(i):
        way = i % 2
        part = chunk(came_from[way], i)
        return remote(part, part, sendr, recvr.at[i], ways[way])

    def strips_of(d):
        return NYC - 1 if d == 0 else NYC

    def arrived(i):
        n = strips_of(ROUND_FIRST[i])
        return remote(
            upd.at[pl.ds(0, n)], all_ref.at[rep, pl.ds(0, n)], send2, recv2.at[i], {"fsdp": me}
        )

    half = BLOCK_SIDE // 2

    def left_piece(k):
        rows = landed[pl.ds(k * NF // 2, NF // 2)].reshape(half, BLOCK_SIDE)
        gram = lax.dot_general(
            rows, landed[...].reshape(BLOCK_SIDE, BLOCK_SIDE), (((1,), (1,)), ((), ())),
            preferred_element_type=f32,
        )
        at = pl.ds(k * half, half)
        nl_ref[0, at, :] = decay_rate * lk[0, at, :] + coef * gram

    def right_piece(k):
        at = pl.ds(k * half, half)
        block = landed[...].reshape(BLOCK_SIDE, BLOCK_SIDE)
        gram = lax.dot_general(
            block[:, k * half:(k + 1) * half], block, (((0,), (0,)), ((), ())),
            preferred_element_type=f32,
        )
        nr_ref[0, at, :] = decay_rate * rk[0, at, :] + coef * gram

    pieces = [lambda: left_piece(0), lambda: left_piece(1), lambda: right_piece(0), lambda: right_piece(1)]

    def work(point):
        for p, at in enumerate(WORK_AT):
            if at == point:
                pieces[p]()

    loads[5].wait()
    loads[6].wait()
    work(-1)
    for k in range(len(OVER_FIRST)):
        for way in range(2):
            over(k, way).wait_recv()
            over_relay(k, way).start()
            group = came_from[way]
            spread(k, group, lambda t: crossed.at[group, k, t])
    count = len(ROUND_FIRST)
    for i in range(count):
        arrived(i).wait_recv()
        own(i, 0).start()
        own(i, 1).start()
        work(i)
        if i >= 1:
            own(i - 1, (i - 1) % 2).wait_recv()
            relay(i - 1).start()
        if i == OPPOSITE_AT:
            for k in range(len(OVER_FIRST)):
                over_relay(k, 0).wait_recv()
                over_relay(k, 1).wait_recv()
                spread(k, opposite, lambda t: crossed.at[opposite, k, t])
    own(count - 1, (count - 1) % 2).wait_recv()
    relay(count - 1).start()
    for i in range(count):
        own(i, 1 - i % 2).wait_recv()
        relay(i).wait_recv()
    if OVER_FIRST:
        n = sum(strips_of(d) for d in OVER_FIRST)
        strips = all_ref.at[:, pl.ds(0, n)]
        whole = remote(strips, strips, send_s, recv_s, {"fsdp": me})
        whole.wait_recv()
        whole.wait_send()

    whole1.wait_send()
    n = sum(strips_of(d) for d in ROUND_FIRST)
    remote(
        upd.at[pl.ds(0, n)], all_ref.at[rep, pl.ds(0, n)], send2, recv2.at[0], {"fsdp": me}
    ).wait_send()
    for k in range(len(OVER_FIRST)):
        for way in range(2):
            over(k, way).wait_send()
            over_relay(k, way).wait_send()
    for i in range(count):
        own(i, 0).wait_send()
        own(i, 1).wait_send()
        relay(i).wait_send()


def finish_kernel(pos_ref, all_ref, nl_ref, nr_ref, out_hbm, nl_hbm, nr_hbm, out, pick, sem):
    to_scalars = pltpu.make_async_copy(pos_ref, pick, sem.at[6])
    to_scalars.start()
    copies = [
        pltpu.make_async_copy(nl_ref, nl_hbm, sem.at[0]),
        pltpu.make_async_copy(nr_ref, nr_hbm, sem.at[1]),
    ]
    for c in copies:
        c.start()
    to_scalars.wait()
    parts = 4
    n = NBLK // parts
    for p in range(parts):
        @pl.loop(p * n, (p + 1) * n, unroll=8)
        def _(b):
            out[b] = all_ref[pick[0, b]]

        c = pltpu.make_async_copy(
            out.at[pl.ds(p * n, n)], out_hbm.at[pl.ds(p * n, n)], sem.at[2 + p]
        )
        c.start()
        copies.append(c)
    for c in copies:
        c.wait()


def per_device(
    gradient, block_group, block_owner, left_kronecker, right_kronecker, left_root, right_root
):
    vmem = pl.BlockSpec(memory_space=pltpu.VMEM)
    anyspace = pl.BlockSpec(memory_space=pl.ANY)
    strips = (NF, ROWS, BLOCK_SIDE)
    square = (1, BLOCK_SIDE, BLOCK_SIDE)
    everything, nl, nr, position = pl.pallas_call(
        step_kernel,
        out_shape=(
            jax.ShapeDtypeStruct((NREP,) + strips, bf16),
            jax.ShapeDtypeStruct(square, f32),
            jax.ShapeDtypeStruct(square, f32),
            jax.ShapeDtypeStruct((1, NBLK), jnp.int32),
        ),
        in_specs=[anyspace] * 7,
        out_specs=(vmem,) * 4,
        scratch_shapes=[
            pltpu.VMEM((1, NBLK), jnp.int32),
            pltpu.VMEM((1, NBLK), jnp.int32),
            pltpu.VMEM((1, 128), jnp.int32),
            pltpu.SMEM((1, 128), jnp.int32),
            pltpu.VMEM((NBLK, ROWS, BLOCK_SIDE), bf16),
            pltpu.VMEM(strips, bf16),
            pltpu.VMEM(strips, bf16),
            pltpu.VMEM(square, f32),
            pltpu.VMEM(square, f32),
            pltpu.VMEM(square, bf16),
            pltpu.VMEM(square, bf16),
            pltpu.VMEM(strips, bf16),
            DMA((8,)),
            DMA, DMA,
            DMA, DMA((NZ,)),
            DMA, DMA((NZ, 2)),
            DMA, DMA((NZ,)),
            pltpu.VMEM((NREP, NZ, NYC, ROWS, BLOCK_SIDE), bf16),
            DMA, DMA((NZ, 2)),
            DMA, DMA((NZ, 2)),
            DMA, DMA,
        ],
        name="shampoo_step",
        cost_estimate=pl.CostEstimate(
            flops=8 * BLOCK_SIDE**3, bytes_accessed=8 << 20, transcendentals=0
        ),
        compiler_params=pltpu.CompilerParams(
            collective_id=0, has_side_effects=True, vmem_limit_bytes=32 << 20
        ),
    )(*[
        pltpu.with_memory_space_constraint(x, pltpu.HBM)
        for x in (
            block_group.reshape(1, NBLK), block_owner.reshape(1, NBLK), gradient,
            left_kronecker, right_kronecker, left_root, right_root,
        )
    ])
    update, new_left, new_right = pl.pallas_call(
        finish_kernel,
        out_shape=(
            jax.ShapeDtypeStruct((NBLK, ROWS, BLOCK_SIDE), bf16),
            jax.ShapeDtypeStruct(square, f32),
            jax.ShapeDtypeStruct(square, f32),
        ),
        in_specs=[vmem] * 4,
        out_specs=(anyspace,) * 3,
        scratch_shapes=[
            pltpu.VMEM((NBLK, ROWS, BLOCK_SIDE), bf16),
            pltpu.SMEM((1, NBLK), jnp.int32),
            DMA((7,)),
        ],
        name="place_update",
        compiler_params=pltpu.CompilerParams(vmem_limit_bytes=40 << 20),
    )(position, everything.reshape(NREP * NF, ROWS, BLOCK_SIDE), nl, nr)
    return (new_left, new_right, update)


def solution(mesh):
    in_specs = (
        P(None, "fsdp", None),
        P(),
        P(),
        P(("rep", "fsdp"), None, None),
        P(("rep", "fsdp"), None, None),
        P(("rep", "fsdp"), None, None),
        P(("rep", "fsdp"), None, None),
    )
    out_specs = (
        P(("rep", "fsdp"), None, None),
        P(("rep", "fsdp"), None, None),
        P(None, "fsdp", None),
    )
    return jax.shard_map(
        per_device, mesh=mesh, in_specs=in_specs, out_specs=out_specs, check_vma=False
    )
```

```python
import jax
import jax.numpy as jnp
from jax import lax
from jax.experimental import pallas as pl
from jax.experimental.pallas import tpu as pltpu
from jax.sharding import PartitionSpec as P

BLOCK_SIDE = 512
NREP = 4
NZ = 8
NY = 4
NCORE = 2
NYC = NY * NCORE
NF = NZ * NYC
ROWS = 8
NBLK = 192

decay_rate = 0.9
epsilon = 1e-06
MESH = pl.DeviceIdType.MESH
DMA = pltpu.SemaphoreType.DMA
bf16 = jnp.bfloat16
f32 = jnp.float32

FIRST_ORDER = (4, 3, 5, 2, 6, 1, 7, 0)
OVER_FIRST = (1, 7, 0)
ROUND_FIRST = ((2, 6), (3, 5), (4,))
Y_ORDER = (0, 1, 3, 2)
SEND_ORDER = tuple((d, e) for together in ROUND_FIRST for d in together for e in Y_ORDER)
LAG = 8
SPREAD_OWN_FIRST = False
OPPOSITE_AT = 10
WORK_AT = (-1, -1, -1, -1)


def step_kernel(
    group_hbm, owner_hbm, grad_hbm, lk_hbm, rk_hbm, lroot_hbm, rroot_hbm,
    all_ref, nl_ref, nr_ref, pos_ref,
    group, owner, source_row, source,
    grad, outgoing, landed, lk, rk, lroot, rroot, upd,
    in_sem, send1, recv1, send2, recv2, sendx, recvx, sendr, recvr,
    crossed, send_o, recv_o, send_or, recv_or, send_s, recv_s,
):
    rep = lax.axis_index("rep")
    me = lax.axis_index("fsdp")
    z = me // NYC
    yc = me % NYC
    y = yc // NCORE
    core = yc % NCORE
    right = (rep + 1) % NREP
    left = (rep + NREP - 1) % NREP

    barrier = pltpu.get_barrier_semaphore()


    for peer in (left, right):
        pl.semaphore_signal(barrier, inc=1, device_id={"rep": peer}, device_id_type=MESH)

    @pl.loop(1, NF)
    def _(s):
        pl.semaphore_signal(
            barrier, inc=1, device_id={"fsdp": lax.rem(me + s, NF)}, device_id_type=MESH
        )

    pairs = (
        (group_hbm, group), (owner_hbm, owner), (grad_hbm, grad),
        (lroot_hbm, lroot), (rroot_hbm, rroot), (lk_hbm, lk), (rk_hbm, rk),
    )
    loads = [pltpu.make_async_copy(a, b, in_sem.at[i]) for i, (a, b) in enumerate(pairs)]
    for load in loads[:3]:
        load.start()
    loads[0].wait()
    loads[1].wait()

    key = group[...] * NF + owner[...]
    c = lax.broadcasted_iota(jnp.int32, (NBLK, NBLK), 0)
    b = lax.broadcasted_iota(jnp.int32, (NBLK, NBLK), 1)
    key_column = jnp.sum(jnp.where(b == c, key, 0), axis=1, keepdims=True)
    rank = jnp.sum(jnp.where((key_column == key) & (c < b), 1, 0), axis=0, keepdims=True)
    position = key + rank
    pos_ref[...] = position
    slot = lax.broadcasted_iota(jnp.int32, (NF, NBLK), 0)
    block = lax.broadcasted_iota(jnp.int32, (NF, NBLK), 1)
    match = position == slot + rep * NF
    source_column = jnp.sum(jnp.where(match, block, 0), axis=1, keepdims=True)
    down = lax.broadcasted_iota(jnp.int32, (NF, 128), 0)
    across = lax.broadcasted_iota(jnp.int32, (NF, 128), 1)
    source_row[...] = jnp.sum(jnp.where(down == across, source_column, 0), axis=0, keepdims=True)
    to_scalars = pltpu.make_async_copy(source_row, source, in_sem.at[7])
    to_scalars.start()
    present = jnp.sum(jnp.where(position == rep * NF + me, 1, 0), axis=1, keepdims=True)
    coef = jnp.where(present > 0, (1.0 - decay_rate) / BLOCK_SIDE, 0.0).astype(f32)
    to_scalars.wait()
    loads[2].wait()

    @pl.loop(0, NF, unroll=8)
    def _(o):
        outgoing[o] = grad[source[0, o]]

    pl.semaphore_wait(barrier, NF + 1)

    @pl.loop(0, NYC)
    def _(j):
        for d in FIRST_ORDER:
            target = lax.rem(z + d, NZ) * NYC + lax.rem(yc + j, NYC)

            def go():
                pltpu.make_async_remote_copy(
                    src_ref=outgoing.at[target], dst_ref=landed.at[me],
                    send_sem=send1, recv_sem=recv1,
                    device_id={"fsdp": target}, device_id_type=MESH,
                ).start()

            if d == 0:
                pl.when(j > 0)(go)
            else:
                go()

    for load in loads[3:]:
        load.start()
    landed[me] = outgoing[me]
    loads[3].wait()
    loads[4].wait()
    whole1 = pltpu.make_async_remote_copy(
        src_ref=outgoing.at[pl.ds(0, NF - 1)], dst_ref=landed.at[pl.ds(0, NF - 1)],
        send_sem=send1, recv_sem=recv1, device_id={"fsdp": me}, device_id_type=MESH,
    )
    whole1.wait_recv()

    g = landed[...].reshape(BLOCK_SIDE, BLOCK_SIDE)
    partial = jnp.dot(lroot[0], g, preferred_element_type=f32).astype(bf16)
    precond = jnp.dot(partial, rroot[0], preferred_element_type=f32)
    wide = g.astype(f32)
    grad_norm = jnp.sqrt(jnp.sum(wide * wide, keepdims=True))
    precond_norm = jnp.sqrt(jnp.sum(precond * precond, keepdims=True) + epsilon)
    update = (precond * (grad_norm / precond_norm)).astype(bf16)
    upd[...] = update.reshape(NF, ROWS, BLOCK_SIDE)

    def remote(src, dst, send, recv, device):
        return pltpu.make_async_remote_copy(
            src_ref=src, dst_ref=dst, send_sem=send, recv_sem=recv,
            device_id=device, device_id_type=MESH,
        )

    ways = ({"rep": right}, {"rep": left})
    came_from = (left, right)
    opposite = (rep + 2) % NREP

    def plane_of(d):
        return lax.rem(z + d, NZ)

    def over(k, way):
        return remote(
            upd.at[pl.ds(plane_of(OVER_FIRST[k]) * NYC, NYC)], crossed.at[rep, k],
            send_o, recv_o.at[k, way], ways[way],
        )

    def over_relay(k, way):
        part = crossed.at[came_from[way], k, pl.ds(way * (NYC // 2), NYC // 2)]
        return remote(part, part, send_or, recv_or.at[k, way], ways[way])

    def spread(k, group, strip):
        d = OVER_FIRST[k]

        @pl.loop(0, NYC)
        def _(j):
            t = lax.rem(yc + j, NYC)

            def go():
                remote(
                    strip(t), all_ref.at[group, me], send_s, recv_s,
                    {"fsdp": plane_of(d) * NYC + t},
                ).start()

            if d == 0:
                pl.when(j > 0)(go)
            else:
                go()

        if d == 0:
            all_ref[group, me] = strip(yc)[...]

    def spread_own():
        for k in range(len(OVER_FIRST)):
            spread(k, rep, lambda t: upd.at[plane_of(OVER_FIRST[k]) * NYC + t])

    for k in range(len(OVER_FIRST)):
        over(k, 0).start()
        over(k, 1).start()

    if SPREAD_OWN_FIRST:
        spread_own()

    pairs = [(d, e) for together in ROUND_FIRST for e in Y_ORDER for d in together]
    for n, (d, e) in enumerate(SEND_ORDER):
        for c in range(NCORE):
            target = plane_of(d) * NYC + lax.rem(y + e, NY) * NCORE + (core + c) % NCORE
            remote(
                upd.at[target], all_ref.at[rep, me], send2, recv2.at[pairs.index((d, e))],
                {"fsdp": target},
            ).start()

    if not SPREAD_OWN_FIRST:
        spread_own()

    def chunk(group, n):
        d, e = pairs[n]
        start = plane_of(NZ - d) * NYC + lax.rem(y + NY - e, NY) * NCORE
        return all_ref.at[group, pl.ds(start, NCORE)]

    def own(n, way):
        return remote(chunk(rep, n), chunk(rep, n), sendx, recvx.at[n, way], ways[way])

    def relay(n):
        way = n % 2
        part = chunk(came_from[way], n)
        return remote(part, part, sendr, recvr.at[n], ways[way])

    def arrived(n):
        return remote(
            upd.at[pl.ds(0, NCORE)], all_ref.at[rep, pl.ds(0, NCORE)], send2, recv2.at[n],
            {"fsdp": me},
        )

    def strips_of(d):
        return NYC - 1 if d == 0 else NYC

    half = BLOCK_SIDE // 2

    def left_piece(k):
        rows = landed[pl.ds(k * NF // 2, NF // 2)].reshape(half, BLOCK_SIDE)
        gram = lax.dot_general(
            rows, landed[...].reshape(BLOCK_SIDE, BLOCK_SIDE), (((1,), (1,)), ((), ())),
            preferred_element_type=f32,
        )
        at = pl.ds(k * half, half)
        nl_ref[0, at, :] = decay_rate * lk[0, at, :] + coef * gram

    def right_piece(k):
        at = pl.ds(k * half, half)
        block = landed[...].reshape(BLOCK_SIDE, BLOCK_SIDE)
        gram = lax.dot_general(
            block[:, k * half:(k + 1) * half], block, (((0,), (0,)), ((), ())),
            preferred_element_type=f32,
        )
        nr_ref[0, at, :] = decay_rate * rk[0, at, :] + coef * gram

    pieces = [lambda: left_piece(0), lambda: left_piece(1), lambda: right_piece(0), lambda: right_piece(1)]

    def work(point):
        for p, at in enumerate(WORK_AT):
            if at == point:
                pieces[p]()

    loads[5].wait()
    loads[6].wait()
    work(-1)
    for k in range(len(OVER_FIRST)):
        for way in range(2):
            over(k, way).wait_recv()
            over_relay(k, way).start()
            group = came_from[way]
            spread(k, group, lambda t: crossed.at[group, k, t])
    count = len(pairs)

    def pass_back(n):
        own(n, n % 2).wait_recv()
        relay(n).start()

    for n in range(count):
        arrived(n).wait_recv()
        own(n, 0).start()
        own(n, 1).start()
        work(n)
        if n >= LAG:
            pass_back(n - LAG)
        if n == OPPOSITE_AT:
            for k in range(len(OVER_FIRST)):
                over_relay(k, 0).wait_recv()
                over_relay(k, 1).wait_recv()
                spread(k, opposite, lambda t: crossed.at[opposite, k, t])
    for n in range(max(count - LAG, 0), count):
        pass_back(n)
    for n in range(count):
        own(n, 1 - n % 2).wait_recv()
        relay(n).wait_recv()
    if OVER_FIRST:
        n = sum(strips_of(d) for d in OVER_FIRST)
        strips = all_ref.at[:, pl.ds(0, n)]
        whole = remote(strips, strips, send_s, recv_s, {"fsdp": me})
        whole.wait_recv()
        whole.wait_send()

    whole1.wait_send()
    n = NCORE * count
    remote(
        upd.at[pl.ds(0, n)], all_ref.at[rep, pl.ds(0, n)], send2, recv2.at[0], {"fsdp": me}
    ).wait_send()
    for k in range(len(OVER_FIRST)):
        for way in range(2):
            over(k, way).wait_send()
            over_relay(k, way).wait_send()
    for n in range(count):
        own(n, 0).wait_send()
        own(n, 1).wait_send()
        relay(n).wait_send()


def finish_kernel(pos_ref, all_ref, nl_ref, nr_ref, out_hbm, nl_hbm, nr_hbm, out, pick, sem):
    to_scalars = pltpu.make_async_copy(pos_ref, pick, sem.at[6])
    to_scalars.start()
    copies = [
        pltpu.make_async_copy(nl_ref, nl_hbm, sem.at[0]),
        pltpu.make_async_copy(nr_ref, nr_hbm, sem.at[1]),
    ]
    for c in copies:
        c.start()
    to_scalars.wait()
    parts = 4
    n = NBLK // parts
    for p in range(parts):
        @pl.loop(p * n, (p + 1) * n, unroll=8)
        def _(b):
            out[b] = all_ref[pick[0, b]]

        c = pltpu.make_async_copy(
            out.at[pl.ds(p * n, n)], out_hbm.at[pl.ds(p * n, n)], sem.at[2 + p]
        )
        c.start()
        copies.append(c)
    for c in copies:
        c.wait()


def per_device(
    gradient, block_group, block_owner, left_kronecker, right_kronecker, left_root, right_root
):
    vmem = pl.BlockSpec(memory_space=pltpu.VMEM)
    anyspace = pl.BlockSpec(memory_space=pl.ANY)
    strips = (NF, ROWS, BLOCK_SIDE)
    square = (1, BLOCK_SIDE, BLOCK_SIDE)
    everything, nl, nr, position = pl.pallas_call(
        step_kernel,
        out_shape=(
            jax.ShapeDtypeStruct((NREP,) + strips, bf16),
            jax.ShapeDtypeStruct(square, f32),
            jax.ShapeDtypeStruct(square, f32),
            jax.ShapeDtypeStruct((1, NBLK), jnp.int32),
        ),
        in_specs=[anyspace] * 7,
        out_specs=(vmem,) * 4,
        scratch_shapes=[
            pltpu.VMEM((1, NBLK), jnp.int32),
            pltpu.VMEM((1, NBLK), jnp.int32),
            pltpu.VMEM((1, 128), jnp.int32),
            pltpu.SMEM((1, 128), jnp.int32),
            pltpu.VMEM((NBLK, ROWS, BLOCK_SIDE), bf16),
            pltpu.VMEM(strips, bf16),
            pltpu.VMEM(strips, bf16),
            pltpu.VMEM(square, f32),
            pltpu.VMEM(square, f32),
            pltpu.VMEM(square, bf16),
            pltpu.VMEM(square, bf16),
            pltpu.VMEM(strips, bf16),
            DMA((8,)),
            DMA, DMA,
            DMA, DMA((NZ * NY,)),
            DMA, DMA((NZ * NY, 2)),
            DMA, DMA((NZ * NY,)),
            pltpu.VMEM((NREP, NZ, NYC, ROWS, BLOCK_SIDE), bf16),
            DMA, DMA((NZ, 2)),
            DMA, DMA((NZ, 2)),
            DMA, DMA,
        ],
        name="shampoo_step",
        cost_estimate=pl.CostEstimate(
            flops=8 * BLOCK_SIDE**3, bytes_accessed=8 << 20, transcendentals=0
        ),
        compiler_params=pltpu.CompilerParams(
            collective_id=0, has_side_effects=True, vmem_limit_bytes=32 << 20
        ),
    )(*[
        pltpu.with_memory_space_constraint(x, pltpu.HBM)
        for x in (
            block_group.reshape(1, NBLK), block_owner.reshape(1, NBLK), gradient,
            left_kronecker, right_kronecker, left_root, right_root,
        )
    ])
    update, new_left, new_right = pl.pallas_call(
        finish_kernel,
        out_shape=(
            jax.ShapeDtypeStruct((NBLK, ROWS, BLOCK_SIDE), bf16),
            jax.ShapeDtypeStruct(square, f32),
            jax.ShapeDtypeStruct(square, f32),
        ),
        in_specs=[vmem] * 4,
        out_specs=(anyspace,) * 3,
        scratch_shapes=[
            pltpu.VMEM((NBLK, ROWS, BLOCK_SIDE), bf16),
            pltpu.SMEM((1, NBLK), jnp.int32),
            DMA((7,)),
        ],
        name="place_update",
        compiler_params=pltpu.CompilerParams(vmem_limit_bytes=40 << 20),
    )(position, everything.reshape(NREP * NF, ROWS, BLOCK_SIDE), nl, nr)
    return (new_left, new_right, update)


def solution(mesh):
    in_specs = (
        P(None, "fsdp", None),
        P(),
        P(),
        P(("rep", "fsdp"), None, None),
        P(("rep", "fsdp"), None, None),
        P(("rep", "fsdp"), None, None),
        P(("rep", "fsdp"), None, None),
    )
    out_specs = (
        P(("rep", "fsdp"), None, None),
        P(("rep", "fsdp"), None, None),
        P(None, "fsdp", None),
    )
    return jax.shard_map(
        per_device, mesh=mesh, in_specs=in_specs, out_specs=out_specs, check_vma=False
    )
```

```python
import jax
import jax.numpy as jnp
from jax import lax
from jax.experimental import pallas as pl
from jax.experimental.pallas import tpu as pltpu
from jax.sharding import PartitionSpec as P

BLOCK_SIDE = 512
NREP = 4
NZ = 8
NY = 4
NCORE = 2
NYC = NY * NCORE
NF = NZ * NYC
ROWS = 8
NBLK = 192

decay_rate = 0.9
epsilon = 1e-06
MESH = pl.DeviceIdType.MESH
DMA = pltpu.SemaphoreType.DMA
bf16 = jnp.bfloat16
f32 = jnp.float32

FIRST_ORDER = (4, 3, 5, 2, 6, 1, 7, 0)
OVER_FIRST = (1, 7, 0)
ROUND_FIRST = ((2, 6), (3, 5), (4,))
Y_ORDER = (0, 1, 3, 2)
SEND_ORDER = tuple((d, e) for together in ROUND_FIRST for d in together for e in Y_ORDER)
LAG = 8
TAKE_AT = (-1, 1, 3)
SPREAD_OWN_FIRST = False
OPPOSITE_AT = 10
WORK_AT = (-1, -1, -1, -1)


def step_kernel(
    group_hbm, owner_hbm, grad_hbm, lk_hbm, rk_hbm, lroot_hbm, rroot_hbm,
    all_ref, nl_ref, nr_ref, pos_ref,
    group, owner, source_row, source,
    grad, outgoing, landed, lk, rk, lroot, rroot, upd,
    in_sem, send1, recv1, send2, recv2, sendx, recvx, sendr, recvr,
    crossed, send_o, recv_o, send_or, recv_or, send_s, recv_s,
):
    rep = lax.axis_index("rep")
    me = lax.axis_index("fsdp")
    z = me // NYC
    yc = me % NYC
    y = yc // NCORE
    core = yc % NCORE
    right = (rep + 1) % NREP
    left = (rep + NREP - 1) % NREP

    barrier = pltpu.get_barrier_semaphore()


    for peer in (left, right):
        pl.semaphore_signal(barrier, inc=1, device_id={"rep": peer}, device_id_type=MESH)

    @pl.loop(1, NF)
    def _(s):
        pl.semaphore_signal(
            barrier, inc=1, device_id={"fsdp": lax.rem(me + s, NF)}, device_id_type=MESH
        )

    pairs = (
        (group_hbm, group), (owner_hbm, owner), (grad_hbm, grad),
        (lroot_hbm, lroot), (rroot_hbm, rroot), (lk_hbm, lk), (rk_hbm, rk),
    )
    loads = [pltpu.make_async_copy(a, b, in_sem.at[i]) for i, (a, b) in enumerate(pairs)]
    for load in loads[:3]:
        load.start()
    loads[0].wait()
    loads[1].wait()

    key = group[...] * NF + owner[...]
    c = lax.broadcasted_iota(jnp.int32, (NBLK, NBLK), 0)
    b = lax.broadcasted_iota(jnp.int32, (NBLK, NBLK), 1)
    key_column = jnp.sum(jnp.where(b == c, key, 0), axis=1, keepdims=True)
    rank = jnp.sum(jnp.where((key_column == key) & (c < b), 1, 0), axis=0, keepdims=True)
    position = key + rank
    pos_ref[...] = position
    slot = lax.broadcasted_iota(jnp.int32, (NF, NBLK), 0)
    block = lax.broadcasted_iota(jnp.int32, (NF, NBLK), 1)
    match = position == slot + rep * NF
    source_column = jnp.sum(jnp.where(match, block, 0), axis=1, keepdims=True)
    down = lax.broadcasted_iota(jnp.int32, (NF, 128), 0)
    across = lax.broadcasted_iota(jnp.int32, (NF, 128), 1)
    source_row[...] = jnp.sum(jnp.where(down == across, source_column, 0), axis=0, keepdims=True)
    to_scalars = pltpu.make_async_copy(source_row, source, in_sem.at[7])
    to_scalars.start()
    present = jnp.sum(jnp.where(position == rep * NF + me, 1, 0), axis=1, keepdims=True)
    coef = jnp.where(present > 0, (1.0 - decay_rate) / BLOCK_SIDE, 0.0).astype(f32)
    to_scalars.wait()
    loads[2].wait()

    @pl.loop(0, NF, unroll=8)
    def _(o):
        outgoing[o] = grad[source[0, o]]

    pl.semaphore_wait(barrier, NF + 1)

    @pl.loop(0, NYC)
    def _(j):
        for d in FIRST_ORDER:
            target = lax.rem(z + d, NZ) * NYC + lax.rem(yc + j, NYC)

            def go():
                pltpu.make_async_remote_copy(
                    src_ref=outgoing.at[target], dst_ref=landed.at[me],
                    send_sem=send1, recv_sem=recv1,
                    device_id={"fsdp": target}, device_id_type=MESH,
                ).start()

            if d == 0:
                pl.when(j > 0)(go)
            else:
                go()

    for load in loads[3:]:
        load.start()
    landed[me] = outgoing[me]
    loads[3].wait()
    loads[4].wait()
    whole1 = pltpu.make_async_remote_copy(
        src_ref=outgoing.at[pl.ds(0, NF - 1)], dst_ref=landed.at[pl.ds(0, NF - 1)],
        send_sem=send1, recv_sem=recv1, device_id={"fsdp": me}, device_id_type=MESH,
    )
    whole1.wait_recv()

    g = landed[...].reshape(BLOCK_SIDE, BLOCK_SIDE)
    partial = jnp.dot(lroot[0], g, preferred_element_type=f32).astype(bf16)
    precond = jnp.dot(partial, rroot[0], preferred_element_type=f32)
    wide = g.astype(f32)
    grad_norm = jnp.sqrt(jnp.sum(wide * wide, keepdims=True))
    precond_norm = jnp.sqrt(jnp.sum(precond * precond, keepdims=True) + epsilon)
    update = (precond * (grad_norm / precond_norm)).astype(bf16)
    upd[...] = update.reshape(NF, ROWS, BLOCK_SIDE)

    def remote(src, dst, send, recv, device):
        return pltpu.make_async_remote_copy(
            src_ref=src, dst_ref=dst, send_sem=send, recv_sem=recv,
            device_id=device, device_id_type=MESH,
        )

    ways = ({"rep": right}, {"rep": left})
    came_from = (left, right)
    opposite = (rep + 2) % NREP

    def plane_of(d):
        return lax.rem(z + d, NZ)

    def over(k, way):
        return remote(
            upd.at[pl.ds(plane_of(OVER_FIRST[k]) * NYC, NYC)], crossed.at[rep, k],
            send_o, recv_o.at[k, way], ways[way],
        )

    def over_relay(k, way):
        part = crossed.at[came_from[way], k, pl.ds(way * (NYC // 2), NYC // 2)]
        return remote(part, part, send_or, recv_or.at[k, way], ways[way])

    def spread(k, group, strip):
        d = OVER_FIRST[k]

        @pl.loop(0, NYC)
        def _(j):
            t = lax.rem(yc + j, NYC)

            def go():
                remote(
                    strip(t), all_ref.at[group, me], send_s, recv_s,
                    {"fsdp": plane_of(d) * NYC + t},
                ).start()

            if d == 0:
                pl.when(j > 0)(go)
            else:
                go()

        if d == 0:
            all_ref[group, me] = strip(yc)[...]

    def spread_own():
        for k in range(len(OVER_FIRST)):
            spread(k, rep, lambda t: upd.at[plane_of(OVER_FIRST[k]) * NYC + t])

    for k in range(len(OVER_FIRST)):
        over(k, 0).start()
        over(k, 1).start()

    if SPREAD_OWN_FIRST:
        spread_own()

    pairs = [(d, e) for together in ROUND_FIRST for e in Y_ORDER for d in together]
    for n, (d, e) in enumerate(SEND_ORDER):
        for c in range(NCORE):
            target = plane_of(d) * NYC + lax.rem(y + e, NY) * NCORE + (core + c) % NCORE
            remote(
                upd.at[target], all_ref.at[rep, me], send2, recv2.at[pairs.index((d, e))],
                {"fsdp": target},
            ).start()

    if not SPREAD_OWN_FIRST:
        spread_own()

    def chunk(group, n):
        d, e = pairs[n]
        start = plane_of(NZ - d) * NYC + lax.rem(y + NY - e, NY) * NCORE
        return all_ref.at[group, pl.ds(start, NCORE)]

    def own(n, way):
        return remote(chunk(rep, n), chunk(rep, n), sendx, recvx.at[n, way], ways[way])

    def relay(n):
        way = n % 2
        part = chunk(came_from[way], n)
        return remote(part, part, sendr, recvr.at[n], ways[way])

    def arrived(n):
        return remote(
            upd.at[pl.ds(0, NCORE)], all_ref.at[rep, pl.ds(0, NCORE)], send2, recv2.at[n],
            {"fsdp": me},
        )

    def strips_of(d):
        return NYC - 1 if d == 0 else NYC

    half = BLOCK_SIDE // 2

    def left_piece(k):
        rows = landed[pl.ds(k * NF // 2, NF // 2)].reshape(half, BLOCK_SIDE)
        gram = lax.dot_general(
            rows, landed[...].reshape(BLOCK_SIDE, BLOCK_SIDE), (((1,), (1,)), ((), ())),
            preferred_element_type=f32,
        )
        at = pl.ds(k * half, half)
        nl_ref[0, at, :] = decay_rate * lk[0, at, :] + coef * gram

    def right_piece(k):
        at = pl.ds(k * half, half)
        block = landed[...].reshape(BLOCK_SIDE, BLOCK_SIDE)
        gram = lax.dot_general(
            block[:, k * half:(k + 1) * half], block, (((0,), (0,)), ((), ())),
            preferred_element_type=f32,
        )
        nr_ref[0, at, :] = decay_rate * rk[0, at, :] + coef * gram

    pieces = [lambda: left_piece(0), lambda: left_piece(1), lambda: right_piece(0), lambda: right_piece(1)]

    def work(point):
        for p, at in enumerate(WORK_AT):
            if at == point:
                pieces[p]()

    loads[5].wait()
    loads[6].wait()
    work(-1)
    def take_over(k):
        for way in range(2):
            over(k, way).wait_recv()
            over_relay(k, way).start()
            group = came_from[way]
            spread(k, group, lambda t: crossed.at[group, k, t])

    for k in range(len(OVER_FIRST)):
        if TAKE_AT[k] < 0:
            take_over(k)
    count = len(pairs)

    def pass_back(n):
        own(n, n % 2).wait_recv()
        relay(n).start()

    for n in range(count):
        arrived(n).wait_recv()
        own(n, 0).start()
        own(n, 1).start()
        work(n)
        for k in range(len(OVER_FIRST)):
            if TAKE_AT[k] == n:
                take_over(k)
        if n >= LAG:
            pass_back(n - LAG)
        if n == OPPOSITE_AT:
            for k in range(len(OVER_FIRST)):
                over_relay(k, 0).wait_recv()
                over_relay(k, 1).wait_recv()
                spread(k, opposite, lambda t: crossed.at[opposite, k, t])
    for n in range(max(count - LAG, 0), count):
        pass_back(n)
    for n in range(count):
        own(n, 1 - n % 2).wait_recv()
        relay(n).wait_recv()
    if OVER_FIRST:
        n = sum(strips_of(d) for d in OVER_FIRST)
        strips = all_ref.at[:, pl.ds(0, n)]
        whole = remote(strips, strips, send_s, recv_s, {"fsdp": me})
        whole.wait_recv()
        whole.wait_send()

    whole1.wait_send()
    n = NCORE * count
    remote(
        upd.at[pl.ds(0, n)], all_ref.at[rep, pl.ds(0, n)], send2, recv2.at[0], {"fsdp": me}
    ).wait_send()
    for k in range(len(OVER_FIRST)):
        for way in range(2):
            over(k, way).wait_send()
            over_relay(k, way).wait_send()
    for n in range(count):
        own(n, 0).wait_send()
        own(n, 1).wait_send()
        relay(n).wait_send()


def finish_kernel(pos_ref, all_ref, nl_ref, nr_ref, out_hbm, nl_hbm, nr_hbm, out, pick, sem):
    to_scalars = pltpu.make_async_copy(pos_ref, pick, sem.at[6])
    to_scalars.start()
    copies = [
        pltpu.make_async_copy(nl_ref, nl_hbm, sem.at[0]),
        pltpu.make_async_copy(nr_ref, nr_hbm, sem.at[1]),
    ]
    for c in copies:
        c.start()
    to_scalars.wait()
    parts = 4
    n = NBLK // parts
    for p in range(parts):
        @pl.loop(p * n, (p + 1) * n, unroll=8)
        def _(b):
            out[b] = all_ref[pick[0, b]]

        c = pltpu.make_async_copy(
            out.at[pl.ds(p * n, n)], out_hbm.at[pl.ds(p * n, n)], sem.at[2 + p]
        )
        c.start()
        copies.append(c)
    for c in copies:
        c.wait()


def per_device(
    gradient, block_group, block_owner, left_kronecker, right_kronecker, left_root, right_root
):
    vmem = pl.BlockSpec(memory_space=pltpu.VMEM)
    anyspace = pl.BlockSpec(memory_space=pl.ANY)
    strips = (NF, ROWS, BLOCK_SIDE)
    square = (1, BLOCK_SIDE, BLOCK_SIDE)
    everything, nl, nr, position = pl.pallas_call(
        step_kernel,
        out_shape=(
            jax.ShapeDtypeStruct((NREP,) + strips, bf16),
            jax.ShapeDtypeStruct(square, f32),
            jax.ShapeDtypeStruct(square, f32),
            jax.ShapeDtypeStruct((1, NBLK), jnp.int32),
        ),
        in_specs=[anyspace] * 7,
        out_specs=(vmem,) * 4,
        scratch_shapes=[
            pltpu.VMEM((1, NBLK), jnp.int32),
            pltpu.VMEM((1, NBLK), jnp.int32),
            pltpu.VMEM((1, 128), jnp.int32),
            pltpu.SMEM((1, 128), jnp.int32),
            pltpu.VMEM((NBLK, ROWS, BLOCK_SIDE), bf16),
            pltpu.VMEM(strips, bf16),
            pltpu.VMEM(strips, bf16),
            pltpu.VMEM(square, f32),
            pltpu.VMEM(square, f32),
            pltpu.VMEM(square, bf16),
            pltpu.VMEM(square, bf16),
            pltpu.VMEM(strips, bf16),
            DMA((8,)),
            DMA, DMA,
            DMA, DMA((NZ * NY,)),
            DMA, DMA((NZ * NY, 2)),
            DMA, DMA((NZ * NY,)),
            pltpu.VMEM((NREP, NZ, NYC, ROWS, BLOCK_SIDE), bf16),
            DMA, DMA((NZ, 2)),
            DMA, DMA((NZ, 2)),
            DMA, DMA,
        ],
        name="shampoo_step",
        cost_estimate=pl.CostEstimate(
            flops=8 * BLOCK_SIDE**3, bytes_accessed=8 << 20, transcendentals=0
        ),
        compiler_params=pltpu.CompilerParams(
            collective_id=0, has_side_effects=True, vmem_limit_bytes=32 << 20
        ),
    )(*[
        pltpu.with_memory_space_constraint(x, pltpu.HBM)
        for x in (
            block_group.reshape(1, NBLK), block_owner.reshape(1, NBLK), gradient,
            left_kronecker, right_kronecker, left_root, right_root,
        )
    ])
    update, new_left, new_right = pl.pallas_call(
        finish_kernel,
        out_shape=(
            jax.ShapeDtypeStruct((NBLK, ROWS, BLOCK_SIDE), bf16),
            jax.ShapeDtypeStruct(square, f32),
            jax.ShapeDtypeStruct(square, f32),
        ),
        in_specs=[vmem] * 4,
        out_specs=(anyspace,) * 3,
        scratch_shapes=[
            pltpu.VMEM((NBLK, ROWS, BLOCK_SIDE), bf16),
            pltpu.SMEM((1, NBLK), jnp.int32),
            DMA((7,)),
        ],
        name="place_update",
        compiler_params=pltpu.CompilerParams(vmem_limit_bytes=40 << 20),
    )(position, everything.reshape(NREP * NF, ROWS, BLOCK_SIDE), nl, nr)
    return (new_left, new_right, update)


def solution(mesh):
    in_specs = (
        P(None, "fsdp", None),
        P(),
        P(),
        P(("rep", "fsdp"), None, None),
        P(("rep", "fsdp"), None, None),
        P(("rep", "fsdp"), None, None),
        P(("rep", "fsdp"), None, None),
    )
    out_specs = (
        P(("rep", "fsdp"), None, None),
        P(("rep", "fsdp"), None, None),
        P(None, "fsdp", None),
    )
    return jax.shard_map(
        per_device, mesh=mesh, in_specs=in_specs, out_specs=out_specs, check_vma=False
    )
```
